32 devices in a mesh: ctx: 4 (over y, x), grp: 8 (over z, core).
Axes of the slice: x: 2, y: 2, z: 4, core: 2. Of those that a mesh axis runs over, the one named last changes fastest.
Arguments:
- tokens: bfloat16 [1024, 6144], P('ctx', 'grp'), may hold values from -6 to 6
- frames: int32 [1024], replicated, may hold values from 0 to 7, never falling along the last dimension, each value on 1 to 512 neighbouring positions
- qkv_weight: bfloat16 [6144, 3072], P(None, 'grp'), may hold values from -0.15309311 to 0.15309311
- out_weight: bfloat16 [1024, 6144], P(None, 'grp'), may hold values from -0.1875 to 0.1875
- cond_weight: bfloat16 [6144, 1536], P('grp'), may hold values from -0.078125 to 0.078125
- cond_bias: float32 [1536], replicated, may hold values from -3 to 3
- in_weight: bfloat16 [16, 1536], replicated, may hold values from -1.5 to 1.5
- mid_weight: bfloat16 [1536, 1536], replicated, may hold values from -0.15625 to 0.15625
- noise_out_weight: bfloat16 [1536, 16], replicated, may hold values from -0.15625 to 0.15625
- head_gain: float32 [1536], replicated, may hold values from 0.5 to 1.5
- targets: float32 [1024, 16], P('ctx'), may hold values from -6 to 6
- noise_draws: float32 [1024, 64], P('ctx'), may hold values from -6 to 6
- timesteps: int32 [1024, 4], P('ctx'), may hold values from 0 to 999
- masked: int32 [1024], P('ctx'), may hold values 0 or 1
- routes: int32 [1024, 1], P('ctx'), may hold values from 0 to 7; in each aligned block of 256 rows (0 to 255, 256 to 511, ...) at most 48 rows name the same one
Outputs:
- hidden_state: bfloat16 [1024, 6144], P('ctx', 'grp')
- predicted_noise: float32 [1536, 64], P(('ctx', 'grp'))
The draws below stay inside these ranges and needn't reach their ends.
Inputs may be any that keep to these rules, and one draw needn't show every extreme that they name: `frames`: frame indices never fall along the clip; each frame has 1 to 512 tokens. `routes`: within the 256 tokens of one index of ctx, at most 48 tokens name any one value, a bound that some block reaches.
All inputs are finite; a program needn't handle non-finite values. No bound on the sum of `masked` on one device may be relied on, other than what follows from the above.
Results may differ from the reference program's by a relative error of at most 0.01.
The reference program's roundings to bfloat16 on the way (of `qkv`, `weights`, `attended`, `noisy`, `normed` and `block`) count: a program that leaves them out, or rounds other values in their place, can miss the bound.
Values may be sent and summed in bfloat16 or wider, within the bound.
A program may use at most 64 MiB of HBM per device.

```python
import math
import jax
import jax.numpy as jnp
import numpy as np
from jax import lax

D = 6144
HD = 128
HEADS = 8
HW = 1536
LAT = 16
DRAWS = 4
TOK_DEV = 256
TOKENS = 1024
CAP = 48
SLOTS = 1536
FRAMES = 8
FRAME_MOST = 512
N_CTX = 4
N_GRP = 8


def draw_qkv_weight(key, part):
    key_entries = jax.random.fold_in(key, 11)
    key_heads = jax.random.fold_in(key, 12)
    entries = jnp.clip(jax.random.normal(key_entries, (D, HEADS, 3, HD), jnp.float32), -2.985, 2.985)
    head_level = jax.random.uniform(key_heads, (HEADS,), jnp.float32)
    head_factor = 4.0 ** head_level
    scaled_cols = jnp.array([1.0, 1.0, 0.0], jnp.float32)
    column_scale = 1.0 + (head_factor[:, None] - 1.0) * scaled_cols[None, :]
    weight = entries * column_scale[None, :, :, None] / math.sqrt(D)
    return weight.reshape(D, HEADS * 3 * HD).astype(jnp.bfloat16)


def place_ends(values, key, least, high):
    spot = [jax.random.randint(jax.random.fold_in(key, axis), (), 0, length) for axis, length in enumerate(values.shape)]
    main_axis = values.shape.index(max(values.shape))
    next_to = spot[:main_axis] + [(spot[main_axis] + 1) % values.shape[main_axis]] + spot[main_axis + 1:]
    return values.at[tuple(spot)].set(least).at[tuple(next_to)].set(high)


def block_scale(key, shape, cuts, smallest, top_value):
    factor_of, own = 1.0, jax.random.fold_in(key, 6)
    for dim, parts in cuts:
        draws = jnp.exp(jax.random.uniform(jax.random.fold_in(own, dim), (parts,), jnp.float32, smallest / len(cuts), top_value / len(cuts)))
        factor_of = factor_of * jnp.repeat(draws, shape[dim] // parts).reshape([-1 if axis == dim else 1 for axis in range(len(shape))])
    return factor_of


def length_profile(number_of, total, bound, slope):
    portions = [(1 << 20) // math.isqrt(standing ** slope) + 1 for standing in range(2, number_of + 1)]
    surplus, given = total - bound - (number_of - 1), [1] * (number_of - 1)
    while surplus > 0:
        free = [i for i in range(number_of - 1) if given[i] < bound]
        pool, remaining = sum([portions[i] for i in free]), surplus
        for i in free:
            extra = min(bound - given[i], max(1, remaining * portions[i] // pool), surplus)
            given[i] = given[i] + extra
            surplus = surplus - extra
    return np.array([bound] + given)


def ragged_sizes(rng, amount, total, most, slope):
    if amount == 2:
        one = jax.random.randint(rng, (), max(1, total - most), min(most, total - 1) + 1)
        return jnp.stack([one, total - one])
    sizes = jnp.asarray(length_profile(amount, total, most, slope), jnp.int32)
    pairs = (amount - 1) // 2
    source_of, sink = sizes[1:1 + 2 * pairs:2], sizes[2:2 + 2 * pairs:2]
    room = jnp.minimum(source_of - 1, most - sink)
    moved = jax.random.randint(jax.random.fold_in(rng, 1), (pairs,), 0, 1 << 20) % (room + 1)
    sizes = sizes.at[1:1 + 2 * pairs:2].set(source_of - moved).at[2:2 + 2 * pairs:2].set(sink + moved)
    return sizes[jax.random.permutation(jax.random.fold_in(rng, 2), amount)]


def routed_block(key, own, number, rows, count, top, most, lean):
    ranking = jax.random.permutation(key, count)
    packed, common = portions_of(count, rows * top, most, lean, True), portions_of(count, rows * top, most, lean, False)
    places = jnp.arange(count)

    def named(tallies, rotation):
        used = int((tallies > 0).sum())
        fixed = max(1, used // 4)
        passed = fixed + (places - fixed + rotation * (used - fixed)) % max(1, count - fixed)
        return jnp.zeros((count,), jnp.int32).at[ranking[jnp.where(places < fixed, places, passed)]].set(jnp.asarray(tallies, jnp.int32))

    tallies = jnp.where(number % 4 == 0, named(packed, number // 4), named(common, number - number // 4 - 1))
    mixed = jax.random.permutation(jax.random.fold_in(own, 3), count)
    source_of, sink = mixed[0:count // 2 * 2:2], mixed[1:count // 2 * 2:2]
    slack = jnp.minimum(tallies[source_of] - 1, most - tallies[sink]) // 2
    slack = jnp.where((source_of == ranking[0]) | (sink == ranking[0]) | (tallies[sink] == 0), 0, jnp.maximum(slack, 0))
    passed = jax.random.randint(jax.random.fold_in(own, 4), (count // 2,), 0, 1 << 20) % (slack + 1)
    tallies = tallies.at[source_of].add(-passed).at[sink].add(passed)
    items = jnp.searchsorted(jnp.cumsum(tallies), jnp.arange(rows * top), side="right").astype(jnp.int32)
    grid = items.reshape(top, rows).T
    grid = grid[jax.random.permutation(jax.random.fold_in(own, 1), rows)]
    rotation = jax.random.randint(jax.random.fold_in(own, 2), (rows, 1), 0, top)
    return jnp.take_along_axis(grid, (jnp.arange(top)[None, :] + rotation) % top, axis=1)


def portions_of(count, total, bound, skew, full):
    weights = [(1 << 20) // math.isqrt(grade ** skew) + 1 for grade in range(1, count + 1)]
    largest = bound if full else min(bound, max(-(-total // count), total * weights[0] // sum(weights)))
    least = 1 if total - largest >= count - 1 else 0
    counts, rest = [largest] + [least] * (count - 1), total - largest - least * (count - 1)
    while rest > 0:
        candidates = [i for i in range(1, count) if counts[i] < largest] or [i for i in range(1, count) if counts[i] < bound]
        whole, left = sum([weights[i] for i in candidates]), rest
        for i in candidates:
            addition = min(bound - counts[i], max(1, left * weights[i] // whole), rest)
            counts[i] = counts[i] + addition
            rest = rest - addition
    return np.array(counts)


def bell_draw(stream_key, shape, scale, bound, shards=(), kind=jnp.bfloat16):
    drawn = jax.random.normal(stream_key, shape, jnp.float32) * scale
    if len(shards) > 0:
        drawn = block_scale(stream_key, shape, shards, -0.22, 0.18) * drawn
    return jnp.clip(drawn, min=-bound, max=bound).astype(kind)


def setup_inputs(seed: int = 0) -> dict:
    seeds = jax.random.split(jax.random.key(seed), 16)
    tokens = bell_draw(seeds[0], (TOKENS, D), 1.0, 6.0, ((0, 4), (1, 8)))
    frames = jnp.searchsorted(jnp.cumsum(ragged_sizes(seeds[1], FRAMES, TOKENS, FRAME_MOST, 0)), jnp.arange(TOKENS), side="right").astype(jnp.int32)
    qkv_weight = draw_qkv_weight(jax.random.fold_in(seeds[15], 71), 0)
    out_weight = bell_draw(seeds[3], (HEADS * HD, D), (HEADS * HD) ** -0.5, 0.1875, ((1, 8),))
    cond_weight = bell_draw(seeds[4], (D, HW), D ** -0.5, 0.078125, ((0, 8),))
    cond_bias = bell_draw(seeds[5], (HW,), 0.5, 3.0, (), jnp.float32)
    in_weight = bell_draw(seeds[6], (LAT, HW), LAT ** -0.5, 1.5)
    mid_weight = bell_draw(seeds[7], (HW, HW), HW ** -0.5, 0.15625)
    noise_out_weight = bell_draw(seeds[8], (HW, LAT), HW ** -0.5, 0.15625)
    head_gain = jnp.clip(1.0 + 0.1 * jax.random.normal(seeds[9], (HW,), jnp.float32), 0.5, 1.5)
    targets = bell_draw(seeds[10], (TOKENS, LAT), 1.0, 6.0, ((0, 4),), jnp.float32)
    noise_draws = bell_draw(seeds[11], (TOKENS, DRAWS * LAT), 1.0, 6.0, ((0, 4),), jnp.float32)
    timesteps = place_ends(jax.random.randint(seeds[12], (TOKENS, DRAWS), 0, 1000), jax.random.fold_in(seeds[12], 1), 0, 999).astype(jnp.int32)
    masked = place_ends((jax.random.randint(seeds[13], (TOKENS,), 0, 4) < 3).astype(jnp.int32), jax.random.fold_in(seeds[13], 1), 0, 1)
    routes_keys = jax.random.split(jax.random.fold_in(seeds[14], 1), TOKENS // TOK_DEV)
    routes_turns = jax.random.permutation(jax.random.fold_in(seeds[14], 3), TOKENS // TOK_DEV)
    routes = jax.vmap(lambda own, number: routed_block(jax.random.fold_in(seeds[14], 2), own, number, TOK_DEV, N_GRP, 1, CAP, 2))(routes_keys, routes_turns).reshape((TOKENS, 1))
    return dict(tokens=tokens, frames=frames, qkv_weight=qkv_weight, out_weight=out_weight, cond_weight=cond_weight, cond_bias=cond_bias, in_weight=in_weight, mid_weight=mid_weight, noise_out_weight=noise_out_weight, head_gain=head_gain, targets=targets, noise_draws=noise_draws, timesteps=timesteps, masked=masked, routes=routes)


def alpha_bar(steps_float):
    return jnp.cos((steps_float / 1000.0 + 0.008) / 1.008 * (math.pi / 2)) ** 2

def time_embed(steps_float, width):
    half_width = width // 2
    freqs = jnp.exp(-math.log(10000.0) * jnp.arange(half_width, dtype=jnp.float32) / half_width)
    angles = steps_float[..., None] * freqs
    return jnp.concatenate([jnp.cos(angles), jnp.sin(angles)], axis=-1)

def head_rows(conditioning, target_rows, noise_rows, steps_float, in_weight, mid_weight, noise_out_weight, head_gain):
    count = conditioning.shape[0]
    latent = target_rows.shape[1]
    draws_count = steps_float.shape[1]
    width = in_weight.shape[1]
    abar = alpha_bar(steps_float)[..., None]
    noisy = jnp.sqrt(abar) * target_rows[:, None, :] + jnp.sqrt(1.0 - abar) * noise_rows.reshape(count, draws_count, latent)
    noisy = noisy.astype(jnp.bfloat16).reshape(count * draws_count, latent)
    lifted = jnp.dot(noisy, in_weight, preferred_element_type=jnp.float32).reshape(count, draws_count, width)
    lifted = lifted + conditioning[:, None, :] + time_embed(steps_float, width)
    scale = lax.rsqrt(lax.optimization_barrier(jnp.mean(lifted * lifted, axis=-1, keepdims=True)) + 1e-06)
    normed = (lifted * scale * head_gain).astype(jnp.bfloat16).reshape(count * draws_count, width)
    middle = jnp.dot(normed, mid_weight, preferred_element_type=jnp.float32)
    block = (lifted.reshape(count * draws_count, width) + jax.nn.silu(middle)).astype(jnp.bfloat16)
    result = jnp.dot(block, noise_out_weight, preferred_element_type=jnp.float32)
    return result.reshape(count, draws_count * latent)

def reference(tokens, frames, qkv_weight, out_weight, cond_weight, cond_bias, in_weight, mid_weight, noise_out_weight, head_gain, targets, noise_draws, timesteps, masked, routes):
    total_rows = tokens.shape[0]
    head_count = qkv_weight.shape[1] // (3 * HD)
    qkv = jnp.dot(tokens, qkv_weight, preferred_element_type=jnp.float32).astype(jnp.bfloat16)
    qkv = qkv.reshape(total_rows, head_count, 3, HD)
    allowed = frames[None, :] <= frames[:, None]

    def one_head(head_index):
        part = lax.dynamic_index_in_dim(qkv, head_index, 1, keepdims=False)
        queries = part[:, 0]
        keys_here = part[:, 1]
        values_here = part[:, 2]
        scores = jnp.dot(queries, keys_here.T, preferred_element_type=jnp.float32) * HD ** (-0.5)
        scores = jnp.where(allowed, scores, -1e+30)
        row_max = lax.optimization_barrier(jnp.max(scores, axis=1, keepdims=True))
        weights = jnp.where(allowed, jnp.exp(scores - row_max), 0.0)
        row_total = lax.optimization_barrier(jnp.sum(weights, axis=1, keepdims=True))
        summed = jnp.dot(weights.astype(jnp.bfloat16), values_here, preferred_element_type=jnp.float32)
        return (summed / row_total).astype(jnp.bfloat16)
    per_head = lax.map(one_head, jnp.arange(head_count, dtype=jnp.int32))
    attended = jnp.transpose(per_head, (1, 0, 2)).reshape(total_rows, head_count * HD)
    projected = jnp.dot(attended, out_weight, preferred_element_type=jnp.float32)
    hidden_state = (tokens.astype(jnp.float32) + projected).astype(jnp.bfloat16)
    conditioning = jnp.dot(hidden_state, cond_weight, preferred_element_type=jnp.float32) + cond_bias
    steps_float = timesteps.astype(jnp.float32)
    predictions = head_rows(conditioning, targets, noise_draws, steps_float, in_weight, mid_weight, noise_out_weight, head_gain)
    target_dev = routes[:, 0]
    onehot = (target_dev[:, None] == jnp.arange(N_GRP, dtype=jnp.int32)[None, :]).astype(jnp.int32) * masked[:, None]
    blocked = onehot.reshape(N_CTX, TOK_DEV, N_GRP)
    before = (jnp.cumsum(blocked, axis=1) - blocked).reshape(total_rows, N_GRP)
    slot_rank = lax.optimization_barrier(jnp.sum(before * onehot, axis=1))
    block_index = (jnp.arange(total_rows, dtype=jnp.int32) // TOK_DEV).astype(jnp.int32)
    slot_index = (block_index * N_GRP + target_dev) * CAP + slot_rank
    slot_index = jnp.where(masked == 1, slot_index, SLOTS).astype(jnp.int32)
    predicted_noise = jnp.zeros((SLOTS, predictions.shape[1]), jnp.float32).at[slot_index].set(predictions, mode='drop')
    return (hidden_state, predicted_noise)
```

```python
import functools
import math

import jax
import jax.numpy as jnp
import numpy as np
from jax import lax
from jax.experimental import pallas as pl
from jax.experimental.pallas import tpu as pltpu
from jax.sharding import PartitionSpec as P

MESH = pl.DeviceIdType.MESH
F32 = jnp.float32
BF16 = jnp.bfloat16
ROW_PARTS = 2


def dot(a, b):
    return jnp.dot(a, b, preferred_element_type=F32)


def kernel(
    n_ctx,
    n_grp,
    cap,
    rows_cap,
    tokens,
    frames,
    qkv_w,
    out_w,
    cond_w,
    bias,
    in_w,
    mid_w,
    noise_out,
    gain,
    targets,
    noise,
    steps,
    masked,
    routes,
    freqs,
    hid_out,
    pred_out,
    tok_all,
    qkv_wv,
    out_wv,
    cond_wv,
    mid_wv,
    kv_all,
    q_own,
    att_all,
    hid,
    acc,
    base,
    normed,
    slot_row,
    mine,
    sib_send,
    sib_recv,
    rs_send,
    rs_recv,
    load_sem,
    up_s,
    up_r,
    fw_s,
    fw_r,
    kv_s,
    kv_r,
    at_s,
    at_r,
    af_s,
    af_r,
    sb_s,
    sb_r,
    rs_s,
    rs_r,
):
    ctx = lax.axis_index("ctx")
    grp = lax.axis_index("grp")
    pairs = n_grp // 2
    pair, core = grp // 2, grp % 2
    sibling = grp + 1 - 2 * core
    tok_rows, d_shard = tokens.shape
    head = q_own.shape[1]
    width = in_w.shape[1]
    latent = targets.shape[1]
    draws = steps.shape[1]
    part = tok_rows // ROW_PARTS
    col = width // rs_s.shape[0]
    n_cols = rs_s.shape[0]

    def remote(src, dst, send, recv, to):
        return pltpu.make_async_remote_copy(
            src_ref=src, dst_ref=dst, send_sem=send, recv_sem=recv, device_id=to, device_id_type=MESH
        )

    def same_core(offset):
        return ((pair + offset + pairs) % pairs) * 2 + core

    loads = [
        pltpu.make_async_copy(src, dst, load_sem.at[i])
        for i, (src, dst) in enumerate(
            (
                (tokens, tok_all.at[grp]),
                (qkv_w, qkv_wv),
                (out_w, out_wv),
                (cond_w, cond_wv),
                (mid_w, mid_wv),
            )
        )
    ]
    loads[0].start()

    barrier = pltpu.get_barrier_semaphore()
    peers = [(ctx, same_core(j)) for j in range(1, pairs)]
    peers += [(ctx, sibling)]
    peers += [((ctx + j) % n_ctx, grp) for j in range(1, n_ctx)]
    for peer in peers:
        pl.semaphore_signal(barrier, inc=1, device_id=peer, device_id_type=MESH)
    for load in loads[1:]:
        load.start()
    pl.semaphore_wait(barrier, len(peers))
    loads[0].wait()

    def piece(shard, k):
        return tok_all.at[shard, pl.ds(k * part, part)]

    def chain(way, step, k):
        sign = 1 if way == 0 else -1
        shard = jnp.clip(pair - sign * step, 0, pairs - 1) * 2 + core
        to = jnp.clip(pair + sign, 0, pairs - 1) * 2 + core
        ref = piece(shard, k)
        return remote(ref, ref, up_s.at[way, step, k], up_r.at[way, step, k], (ctx, to))

    def chain_in(way, step, k):
        sign = 1 if way == 0 else -1
        shard = jnp.clip(pair - sign * (step + 1), 0, pairs - 1) * 2 + core
        ref = piece(shard, k)
        return remote(ref, ref, up_s.at[way, step, k], up_r.at[way, step, k], (ctx, sibling))

    def sends(way, step):
        if way == 0:
            return (pair - step >= 0) & (pair + 1 < pairs)
        return (pair + step < pairs) & (pair >= 1)

    def gets(way, step):
        if way == 0:
            return pair - 1 - step >= 0
        return pair + 1 + step < pairs

    def forward(way, step, k, from_sibling=False):
        sign = 1 if way == 0 else -1
        shard = jnp.clip(pair - sign * step, 0, pairs - 1) * 2 + (1 - core if from_sibling else core)
        ref = piece(shard, k)
        return remote(ref, ref, fw_s.at[way, step, k], fw_r.at[way, step, k], (ctx, sibling))

    for k in range(ROW_PARTS):
        for way in (0, 1):

            @pl.when(sends(way, 0))
            def _():
                chain(way, 0, k).start()

    for k in range(ROW_PARTS):
        forward(0, 0, k).start()

    def add_qkv(shard, k, first=False):
        weight = qkv_wv[pl.ds(pl.multiple_of(shard * d_shard, d_shard), d_shard), :]
        rows = pl.ds(k * part, part)
        term = dot(tok_all[shard, k * part : (k + 1) * part, :], weight)
        acc[rows, :] = term if first else acc[rows, :] + term

    def slots_of():
        mask = masked[...]
        route = routes[...]
        shape = (n_grp, tok_rows)
        onehot = jnp.where((lax.broadcasted_iota(jnp.int32, shape, 0) == route) & (mask == 1), 1.0, 0.0)
        square = (tok_rows, tok_rows)
        earlier = lax.broadcasted_iota(jnp.int32, square, 0) < lax.broadcasted_iota(jnp.int32, square, 1)
        before = dot(onehot.astype(BF16), jnp.where(earlier, 1.0, 0.0).astype(BF16))
        rank = jnp.sum(before * onehot, axis=0, keepdims=True).astype(jnp.int32)
        slot_row[...] = jnp.where(mask == 1, route * rows_cap + rank, -1)

    def own_slots():
        want = lax.broadcasted_iota(jnp.int32, (rows_cap, tok_rows), 0) + grp * rows_cap
        return jnp.where(want == slot_row[...], 1.0, 0.0)

    def draw_base(k):
        own = own_slots().astype(BF16)
        step = steps[:, k : k + 1]
        stepf = step.astype(F32)
        abar = jnp.cos((stepf / 1000.0 + 0.008) / 1.008 * (math.pi / 2)) ** 2
        lanes = slice(k * latent, (k + 1) * latent)
        noisy = (jnp.sqrt(abar) * targets[...] + jnp.sqrt(1.0 - abar) * noise[:, lanes]).astype(BF16)
        picked = dot(own, noisy).astype(BF16)
        high = (step >> 5).astype(F32)
        low = (step & 31).astype(F32)
        s = dot(own, high.astype(BF16)) * 32.0 + dot(own, low.astype(BF16))
        rows = slice(k * rows_cap, (k + 1) * rows_cap)
        angles = s * freqs[...]
        half = width // 2
        base[rows, :half] = dot(picked, in_w[:, :half]) + jnp.cos(angles) + bias[:, :half]
        base[rows, half:] = dot(picked, in_w[:, half:]) + jnp.sin(angles) + bias[:, half:]

    work = [functools.partial(draw_base, k) for k in range(draws)]
    slots_of()
    loads[1].wait()
    for k in range(ROW_PARTS):
        add_qkv(grp, k, first=True)

    for step in range(pairs - 1):
        for k in range(ROW_PARTS):
            for way in (0, 1):

                @pl.when(gets(way, step))
                def _():
                    chain_in(way, step, k).wait_recv()

                if step + 1 < pairs - 1:

                    @pl.when(sends(way, step + 1))
                    def _():
                        chain(way, step + 1, k).start()

                @pl.when(gets(way, step))
                def _():
                    forward(way, step + 1, k).start()
                    sign = 1 if way == 0 else -1
                    add_qkv((pair - sign * (step + 1)) * 2 + core, k)

            for way in (0, 1) if step else (0,):

                @pl.when(True if step == 0 else gets(way, step - 1))
                def _():
                    forward(way, step, k, True).wait_recv()
                    sign = 1 if way == 0 else -1
                    add_qkv((pair - sign * step) * 2 + 1 - core, k)

            if work:
                work.pop(0)()
    while work:
        work.pop(0)()
    for k in range(ROW_PARTS):
        for way in (0, 1):

            @pl.when(gets(way, pairs - 2))
            def _():
                forward(way, pairs - 1, k, True).wait_recv()
                sign = 1 if way == 0 else -1
                add_qkv((pair - sign * (pairs - 1)) * 2 + 1 - core, k)

    kv_all[0] = acc[:, head:].astype(BF16)
    kv_copies = []
    for j in range(1, n_ctx):
        copy = remote(kv_all.at[0], kv_all.at[j], kv_s.at[j], kv_r.at[j], ((ctx + j) % n_ctx, grp))
        copy.start()
        kv_copies.append(copy)
    q = acc[:, :head].astype(BF16)
    mine_frames = frames[:, pl.ds(pl.multiple_of(ctx * tok_rows, tok_rows), tok_rows)]
    square = (tok_rows, tok_rows)
    same = lax.broadcasted_iota(jnp.int32, square, 0) == lax.broadcasted_iota(jnp.int32, square, 1)
    frame_col = jnp.sum(jnp.where(same, mine_frames, 0), axis=1, keepdims=True)
    scores = []
    for j in range(n_ctx):
        if j:
            kv_copies[j - 1].wait_recv()
        block = (ctx + n_ctx - j) % n_ctx
        frame_row = frames[:, pl.ds(pl.multiple_of(block * tok_rows, tok_rows), tok_rows)]
        s = lax.dot_general(
            q, kv_all[j, :, :head], (((1,), (1,)), ((), ())), preferred_element_type=F32
        ) * (head**-0.5)
        scores.append(jnp.where(frame_row <= frame_col, s, -1e30))
    top = functools.reduce(jnp.maximum, [jnp.max(s, axis=1, keepdims=True) for s in scores])
    total = jnp.zeros((tok_rows, 1), F32)
    weighted = jnp.zeros((tok_rows, head), F32)
    for j in range(n_ctx):
        w = jnp.exp(scores[j] - top)
        total = total + jnp.sum(w, axis=1, keepdims=True)
        weighted = weighted + dot(w.astype(BF16), kv_all[j, :, head:])

    def heads(index):
        return att_all.at[:, pl.ds(pl.multiple_of(index * head, head), head)]

    q_own[...] = (weighted / total).astype(BF16)
    att_all[:, pl.ds(pl.multiple_of(grp * head, head), head)] = q_own[...]
    att_copies = []
    for j in range(1, pairs):
        copy = remote(q_own, heads(grp), at_s.at[j], at_r.at[j], (ctx, same_core(j)))
        copy.start()
        att_copies.append(copy)
    att_fw = [remote(q_own, heads(grp), af_s.at[0], af_r.at[0], (ctx, sibling))]
    att_fw[0].start()
    for j in range(1, pairs):
        got = heads(same_core(-j))
        remote(got, got, at_s.at[j], at_r.at[j], (ctx, sibling)).wait_recv()
        copy = remote(got, got, af_s.at[j], af_r.at[j], (ctx, sibling))
        copy.start()
        att_fw.append(copy)
    loads[2].wait()
    for j in range(pairs):
        got = heads(same_core(-j) + 1 - 2 * core)
        remote(got, got, af_s.at[j], af_r.at[j], (ctx, sibling)).wait_recv()
    projected = dot(att_all[...], out_wv[...])
    hidden = (tok_all[grp].astype(F32) + projected).astype(BF16)
    hid_out[...] = hidden
    hid[...] = hidden

    loads[3].wait()
    row = slot_row[...]
    slots_shape = (pairs * rows_cap, tok_rows)
    place = lax.broadcasted_iota(jnp.int32, slots_shape, 0)
    route = routes[...]
    pair_slot = row - route * rows_cap + (route >> 1) * rows_cap
    mine_row = jnp.where((row >= 0) & ((route & 1) == core), pair_slot, -1)
    sib_row = jnp.where((row >= 0) & ((route & 1) != core), pair_slot, -1)
    choose_mine = jnp.where(place == mine_row, 1.0, 0.0).astype(BF16)
    choose_sib = jnp.where(place == sib_row, 1.0, 0.0).astype(BF16)
    sib_copies = []
    for k in range(n_cols):
        cols = slice(k * col, (k + 1) * col)
        by_token = dot(hid[...], cond_wv[:, cols]).astype(BF16)
        sib_send[k] = dot(choose_sib, by_token).astype(BF16)
        copy = remote(sib_send.at[k], sib_recv.at[k], sb_s.at[k], sb_r.at[k], (ctx, sibling))
        copy.start()
        sib_copies.append(copy)
        mine[k] = dot(choose_mine, by_token)
    rs_copies = []
    for k in range(n_cols):
        sib_copies[k].wait_recv()
        summed = mine[k] + sib_recv[k].astype(F32)
        mine[k] = summed
        rs_send[k] = summed.astype(BF16)
        for j in range(1, pairs):
            to = (pair + j) % pairs
            rows = pl.ds(pl.multiple_of(to * rows_cap, rows_cap), rows_cap)
            copy = remote(
                rs_send.at[k, rows], rs_recv.at[k, j], rs_s.at[k, j], rs_r.at[k, j], (ctx, to * 2 + core)
            )
            copy.start()
            rs_copies.append(copy)

    squares = [jnp.zeros((rows_cap, 1), F32) for _ in range(draws)]
    for k in range(n_cols):
        cols = slice(k * col, (k + 1) * col)
        cond = mine[k, pl.ds(pl.multiple_of(pair * rows_cap, rows_cap), rows_cap), :]
        for j in range(1, pairs):
            rs_copies[k * (pairs - 1) + j - 1].wait_recv()
            cond = cond + rs_recv[k, j].astype(F32)
        for d in range(draws):
            rows = slice(d * rows_cap, (d + 1) * rows_cap)
            lifted = base[rows, cols] + cond
            base[rows, cols] = lifted
            squares[d] = squares[d] + jnp.sum(lifted * lifted, axis=1, keepdims=True)
    for d in range(draws):
        rows = slice(d * rows_cap, (d + 1) * rows_cap)
        scale = lax.rsqrt(squares[d] / width + 1e-06)
        normed[rows, :] = (base[rows, :] * scale * gain[...]).astype(BF16)
    loads[4].wait()

    def middle_cols(i, total):
        start = pl.multiple_of(i * 256, 256)
        middle = dot(normed[...], mid_wv[:, pl.ds(start, 256)])
        block = (base[:, pl.ds(start, 256)] + middle / (1.0 + jnp.exp(-middle))).astype(BF16)
        return total + dot(block, noise_out[pl.ds(start, 256), :])

    result = lax.fori_loop(0, width // 256, middle_cols, jnp.zeros((draws * rows_cap, latent), F32))
    occupied = jnp.sum(own_slots(), axis=1, keepdims=True)
    for d in range(draws):
        block = result[d * rows_cap : (d + 1) * rows_cap] * occupied
        pred_out[:, d * latent : (d + 1) * latent] = block[:cap]

    for k in range(ROW_PARTS):
        forward(0, 0, k).wait_send()
        for way in (0, 1):
            for step in range(pairs - 1):

                @pl.when(sends(way, step))
                def _():
                    chain(way, step, k).wait_send()

                @pl.when(gets(way, step))
                def _():
                    forward(way, step + 1, k).wait_send()

    for copy in kv_copies + att_copies + att_fw + sib_copies + rs_copies:
        copy.wait_send()


def shards(n_ctx, n_grp, *arrays):
    (tokens, frames, qkv_w, out_w, cond_w, bias, in_w, mid_w, noise_out, gain) = arrays[:10]
    targets, noise, steps, masked, routes = arrays[10:]
    tok_rows, d_shard = tokens.shape
    head = qkv_w.shape[1] // 3
    width = in_w.shape[1]
    draws = steps.shape[1]
    pairs = n_grp // 2
    cap = max(2, 3 * tok_rows // (2 * n_grp))
    rows_cap = -(-cap // 16) * 16
    n_cols = 3
    col = width // n_cols
    half = width // 2
    freqs = np.exp(-math.log(10000.0) * np.arange(half, dtype=np.float32) / half).astype(np.float32)
    vmem = pl.BlockSpec(memory_space=pltpu.VMEM)
    hbm = pl.BlockSpec(memory_space=pl.ANY)
    dma = pltpu.SemaphoreType.DMA
    chain = dma((2, pairs - 1, ROW_PARTS))
    fwd = dma((2, pairs, ROW_PARTS))
    ops = (
        tokens,
        frames.reshape(1, -1),
        qkv_w,
        out_w,
        cond_w,
        bias.reshape(1, -1),
        in_w,
        mid_w,
        noise_out,
        gain.reshape(1, -1),
        targets,
        noise,
        steps,
        masked.reshape(1, -1),
        routes.reshape(1, -1),
        jnp.asarray(freqs).reshape(1, -1),
    )
    specs = [hbm if i in (0, 2, 3, 4, 7) else vmem for i in range(len(ops))]
    return pl.pallas_call(
        functools.partial(kernel, n_ctx, n_grp, cap, rows_cap),
        out_shape=(
            jax.ShapeDtypeStruct(tokens.shape, BF16),
            jax.ShapeDtypeStruct((cap, noise.shape[1]), F32),
        ),
        in_specs=specs,
        out_specs=(vmem, vmem),
        scratch_shapes=[
            pltpu.VMEM((n_grp, tok_rows, d_shard), BF16),
            pltpu.VMEM(qkv_w.shape, BF16),
            pltpu.VMEM(out_w.shape, BF16),
            pltpu.VMEM(cond_w.shape, BF16),
            pltpu.VMEM(mid_w.shape, BF16),
            pltpu.VMEM((n_ctx, tok_rows, 2 * head), BF16),
            pltpu.VMEM((tok_rows, head), BF16),
            pltpu.VMEM((tok_rows, n_grp * head), BF16),
            pltpu.VMEM((tok_rows, d_shard), BF16),
            pltpu.VMEM((tok_rows, 3 * head), F32),
            pltpu.VMEM((draws * rows_cap, width), F32),
            pltpu.VMEM((draws * rows_cap, width), BF16),
            pltpu.VMEM((1, tok_rows), jnp.int32),
            pltpu.VMEM((n_cols, pairs * rows_cap, col), F32),
            pltpu.VMEM((n_cols, pairs * rows_cap, col), BF16),
            pltpu.VMEM((n_cols, pairs * rows_cap, col), BF16),
            pltpu.VMEM((n_cols, pairs * rows_cap, col), BF16),
            pltpu.VMEM((n_cols, pairs, rows_cap, col), BF16),
            dma((5,)),
            chain,
            chain,
            fwd,
            fwd,
            dma((n_ctx,)),
            dma((n_ctx,)),
            dma((pairs,)),
            dma((pairs,)),
            dma((pairs,)),
            dma((pairs,)),
            dma((n_cols,)),
            dma((n_cols,)),
            dma((n_cols, pairs)),
            dma((n_cols, pairs)),
        ],
        compiler_params=pltpu.CompilerParams(
            collective_id=0, has_side_effects=True, vmem_limit_bytes=52 * 2**20
        ),
    )(*ops)


def solution(mesh):
    return jax.shard_map(
        functools.partial(shards, mesh.shape["ctx"], mesh.shape["grp"]),
        mesh=mesh,
        in_specs=(
            P("ctx", "grp"),
            P(),
            P(None, "grp"),
            P(None, "grp"),
            P("grp", None),
            P(),
            P(),
            P(),
            P(),
            P(),
            P("ctx", None),
            P("ctx", None),
            P("ctx", None),
            P("ctx"),
            P("ctx", None),
        ),
        out_specs=(P("ctx", "grp"), P(("ctx", "grp"), None)),
        check_vma=False,
    )
```

```python
import functools
import math

import jax
import jax.numpy as jnp
import numpy as np
from jax import lax
from jax.experimental import pallas as pl
from jax.experimental.pallas import tpu as pltpu
from jax.sharding import PartitionSpec as P

MESH = pl.DeviceIdType.MESH
F32 = jnp.float32
BF16 = jnp.bfloat16
ROW_PARTS = 2


def dot(a, b):
    return jnp.dot(a, b, preferred_element_type=F32)


def kernel(
    n_ctx,
    n_grp,
    cap,
    rows_cap,
    tokens,
    frames_h,
    qkv_w,
    out_w,
    cond_w,
    bias_h,
    in_w_h,
    mid_w,
    noise_out_h,
    gain_h,
    targets_h,
    noise_h,
    steps_h,
    masked_h,
    routes_h,
    freqs_h,
    hid_out,
    pred_out,
    frames,
    bias_rows,
    in_w,
    noise_out,
    gain_rows,
    targets,
    noise,
    steps,
    masked,
    routes,
    freqs_rows,
    tok_all,
    qkv_wv,
    out_wv,
    cond_wv,
    mid_wv,
    kv_all,
    q_own,
    att_all,
    hid,
    acc,
    base,
    normed,
    step_slots,
    picked,
    slot_row,
    mine,
    sib_send,
    sib_recv,
    rs_send,
    rs_recv,
    load_sem,
    small_sem,
    up_s,
    up_r,
    fw_s,
    fw_r,
    kv_s,
    kv_r,
    at_s,
    at_r,
    af_s,
    af_r,
    sb_s,
    sb_r,
    rs_s,
    rs_r,
):
    ctx = lax.axis_index("ctx")
    grp = lax.axis_index("grp")
    pairs = n_grp // 2
    pair, core = grp // 2, grp % 2
    sibling = grp + 1 - 2 * core
    tok_rows, d_shard = tokens.shape
    head = q_own.shape[1]
    width = in_w.shape[1]
    latent = targets.shape[0]
    draws = steps.shape[0]
    part = tok_rows // ROW_PARTS
    col = width // rs_s.shape[0]
    n_cols = rs_s.shape[0]

    def remote(src, dst, send, recv, to):
        return pltpu.make_async_remote_copy(
            src_ref=src, dst_ref=dst, send_sem=send, recv_sem=recv, device_id=to, device_id_type=MESH
        )

    def same_core(offset):
        return ((pair + offset + pairs) % pairs) * 2 + core

    loads = [
        pltpu.make_async_copy(src, dst, load_sem.at[i])
        for i, (src, dst) in enumerate(
            (
                (tokens, tok_all.at[grp]),
                (qkv_w, qkv_wv),
                (out_w, out_wv),
                (cond_w, cond_wv),
                (mid_w, mid_wv),
            )
        )
    ]
    loads[0].start()
    smalls = [
        pltpu.make_async_copy(src, dst, small_sem.at[i])
        for i, (src, dst) in enumerate(
            (
                (masked_h, masked),
                (routes_h, routes),
                (targets_h, targets),
                (noise_h, noise),
                (steps_h, steps),
                (freqs_h, freqs_rows),
                (in_w_h, in_w),
                (bias_h, bias_rows),
                (frames_h, frames),
                (gain_h, gain_rows),
                (noise_out_h, noise_out),
            )
        )
    ]

    def row_of(ref):
        return jnp.concatenate([ref[i : i + 1, :] for i in range(ref.shape[0])], axis=1)

    barrier = pltpu.get_barrier_semaphore()
    peers = [(ctx, same_core(j)) for j in range(1, pairs)]
    peers += [(ctx, sibling)]
    peers += [((ctx + j) % n_ctx, grp) for j in range(1, n_ctx)]
    for peer in peers:
        pl.semaphore_signal(barrier, inc=1, device_id=peer, device_id_type=MESH)
    for load in loads[1:2] + smalls + loads[2:]:
        load.start()
    pl.semaphore_wait(barrier, len(peers))
    loads[0].wait()

    def piece(shard, k):
        return tok_all.at[shard, pl.ds(k * part, part)]

    def chain(way, step, k):
        sign = 1 if way == 0 else -1
        shard = jnp.clip(pair - sign * step, 0, pairs - 1) * 2 + core
        to = jnp.clip(pair + sign, 0, pairs - 1) * 2 + core
        ref = piece(shard, k)
        return remote(ref, ref, up_s.at[way, step, k], up_r.at[way, step, k], (ctx, to))

    def chain_in(way, step, k):
        sign = 1 if way == 0 else -1
        shard = jnp.clip(pair - sign * (step + 1), 0, pairs - 1) * 2 + core
        ref = piece(shard, k)
        return remote(ref, ref, up_s.at[way, step, k], up_r.at[way, step, k], (ctx, sibling))

    def sends(way, step):
        if way == 0:
            return (pair - step >= 0) & (pair + 1 < pairs)
        return (pair + step < pairs) & (pair >= 1)

    def gets(way, step):
        if way == 0:
            return pair - 1 - step >= 0
        return pair + 1 + step < pairs

    def forward(way, step, k, from_sibling=False):
        sign = 1 if way == 0 else -1
        shard = jnp.clip(pair - sign * step, 0, pairs - 1) * 2 + (1 - core if from_sibling else core)
        ref = piece(shard, k)
        return remote(ref, ref, fw_s.at[way, step, k], fw_r.at[way, step, k], (ctx, sibling))

    for k in range(ROW_PARTS):
        for way in (0, 1):

            @pl.when(sends(way, 0))
            def _():
                chain(way, 0, k).start()

    for k in range(ROW_PARTS):
        forward(0, 0, k).start()

    def add_qkv(shard, k, first=False):
        weight = qkv_wv[pl.ds(pl.multiple_of(shard * d_shard, d_shard), d_shard), :]
        rows = pl.ds(k * part, part)
        term = dot(tok_all[shard, k * part : (k + 1) * part, :], weight)
        acc[rows, :] = term if first else acc[rows, :] + term

    def slots_of():
        mask = masked[...]
        route = routes[...]
        shape = (n_grp, tok_rows)
        onehot = jnp.where((lax.broadcasted_iota(jnp.int32, shape, 0) == route) & (mask == 1), 1.0, 0.0)
        square = (tok_rows, tok_rows)
        earlier = lax.broadcasted_iota(jnp.int32, square, 0) < lax.broadcasted_iota(jnp.int32, square, 1)
        before = dot(onehot.astype(BF16), jnp.where(earlier, 1.0, 0.0).astype(BF16))
        rank = jnp.sum(before * onehot, axis=0, keepdims=True).astype(jnp.int32)
        slot_row[...] = jnp.where(mask == 1, route * rows_cap + rank, -1)

    def own_slots():
        want = lax.broadcasted_iota(jnp.int32, (rows_cap, tok_rows), 0) + grp * rows_cap
        return jnp.where(want == slot_row[...], 1.0, 0.0)

    def noisy_of():
        own = own_slots().astype(BF16)
        step = steps[...]
        pick = (((1,), (1,)), ((), ()))
        high = (step >> 5).astype(F32).astype(BF16)
        low = (step & 31).astype(F32).astype(BF16)
        step_slots[...] = lax.dot_general(
            own, high, pick, preferred_element_type=F32
        ) * 32.0 + lax.dot_general(own, low, pick, preferred_element_type=F32)
        abar = jnp.cos((step.astype(F32) / 1000.0 + 0.008) / 1.008 * (math.pi / 2)) ** 2
        keep, add = jnp.sqrt(abar), jnp.sqrt(1.0 - abar)
        for k in range(draws):
            drawn = noise[k * latent : (k + 1) * latent, :]
            noisy = (keep[k : k + 1] * targets[...] + add[k : k + 1] * drawn).astype(BF16)
            rows = slice(k * rows_cap, (k + 1) * rows_cap)
            picked[rows, :] = lax.dot_general(own, noisy, pick, preferred_element_type=F32).astype(BF16)

    def draw_base(k):
        rows = slice(k * rows_cap, (k + 1) * rows_cap)
        angles = step_slots[:, k : k + 1] * row_of(freqs_rows)
        half = width // 2
        bias = row_of(bias_rows)
        base[rows, :half] = dot(picked[rows, :], in_w[:, :half]) + jnp.cos(angles) + bias[:, :half]
        base[rows, half:] = dot(picked[rows, :], in_w[:, half:]) + jnp.sin(angles) + bias[:, half:]

    work = [noisy_of] + [functools.partial(draw_base, k) for k in range(draws)]
    for load in smalls:
        load.wait()
    slots_of()
    loads[1].wait()
    for k in range(ROW_PARTS):
        add_qkv(grp, k, first=True)

    for step in range(pairs - 1):
        for k in range(ROW_PARTS):
            for way in (0, 1):

                @pl.when(gets(way, step))
                def _():
                    chain_in(way, step, k).wait_recv()

                if step + 1 < pairs - 1:

                    @pl.when(sends(way, step + 1))
                    def _():
                        chain(way, step + 1, k).start()

                @pl.when(gets(way, step))
                def _():
                    forward(way, step + 1, k).start()
                    sign = 1 if way == 0 else -1
                    add_qkv((pair - sign * (step + 1)) * 2 + core, k)

            for way in (0, 1) if step else (0,):

                @pl.when(True if step == 0 else gets(way, step - 1))
                def _():
                    forward(way, step, k, True).wait_recv()
                    sign = 1 if way == 0 else -1
                    add_qkv((pair - sign * step) * 2 + 1 - core, k)

            if work:
                work.pop(0)()
    while work:
        work.pop(0)()
    for k in range(ROW_PARTS):
        for way in (0, 1):

            @pl.when(gets(way, pairs - 2))
            def _():
                forward(way, pairs - 1, k, True).wait_recv()
                sign = 1 if way == 0 else -1
                add_qkv((pair - sign * (pairs - 1)) * 2 + 1 - core, k)

    kv_all[0] = acc[:, head:].astype(BF16)
    kv_copies = []
    for j in range(1, n_ctx):
        copy = remote(kv_all.at[0], kv_all.at[j], kv_s.at[j], kv_r.at[j], ((ctx + j) % n_ctx, grp))
        copy.start()
        kv_copies.append(copy)
    q = acc[:, :head].astype(BF16)
    mine_frames = frames[:, pl.ds(pl.multiple_of(ctx * tok_rows, tok_rows), tok_rows)]
    square = (tok_rows, tok_rows)
    same = lax.broadcasted_iota(jnp.int32, square, 0) == lax.broadcasted_iota(jnp.int32, square, 1)
    frame_col = jnp.sum(jnp.where(same, mine_frames, 0), axis=1, keepdims=True)
    scores = []
    for j in range(n_ctx):
        if j:
            kv_copies[j - 1].wait_recv()
        block = (ctx + n_ctx - j) % n_ctx
        frame_row = frames[:, pl.ds(pl.multiple_of(block * tok_rows, tok_rows), tok_rows)]
        s = lax.dot_general(
            q, kv_all[j, :, :head], (((1,), (1,)), ((), ())), preferred_element_type=F32
        ) * (head**-0.5)
        scores.append(jnp.where(frame_row <= frame_col, s, -1e30))
    top = functools.reduce(jnp.maximum, [jnp.max(s, axis=1, keepdims=True) for s in scores])
    total = jnp.zeros((tok_rows, 1), F32)
    weighted = jnp.zeros((tok_rows, head), F32)
    for j in range(n_ctx):
        w = jnp.exp(scores[j] - top)
        total = total + jnp.sum(w, axis=1, keepdims=True)
        weighted = weighted + dot(w.astype(BF16), kv_all[j, :, head:])

    def heads(index):
        return att_all.at[:, pl.ds(pl.multiple_of(index * head, head), head)]

    q_own[...] = (weighted / total).astype(BF16)
    att_all[:, pl.ds(pl.multiple_of(grp * head, head), head)] = q_own[...]
    att_copies = []
    for j in range(1, pairs):
        copy = remote(q_own, heads(grp), at_s.at[j], at_r.at[j], (ctx, same_core(j)))
        copy.start()
        att_copies.append(copy)
    att_fw = [remote(q_own, heads(grp), af_s.at[0], af_r.at[0], (ctx, sibling))]
    att_fw[0].start()
    for j in range(1, pairs):
        got = heads(same_core(-j))
        remote(got, got, at_s.at[j], at_r.at[j], (ctx, sibling)).wait_recv()
        copy = remote(got, got, af_s.at[j], af_r.at[j], (ctx, sibling))
        copy.start()
        att_fw.append(copy)
    loads[2].wait()
    for j in range(pairs):
        got = heads(same_core(-j) + 1 - 2 * core)
        remote(got, got, af_s.at[j], af_r.at[j], (ctx, sibling)).wait_recv()
    projected = dot(att_all[...], out_wv[...])
    hidden = (tok_all[grp].astype(F32) + projected).astype(BF16)
    hid_out[...] = hidden
    hid[...] = hidden

    loads[3].wait()
    row = slot_row[...]
    slots_shape = (pairs * rows_cap, tok_rows)
    place = lax.broadcasted_iota(jnp.int32, slots_shape, 0)
    route = routes[...]
    pair_slot = row - route * rows_cap + (route >> 1) * rows_cap
    mine_row = jnp.where((row >= 0) & ((route & 1) == core), pair_slot, -1)
    sib_row = jnp.where((row >= 0) & ((route & 1) != core), pair_slot, -1)
    choose_mine = jnp.where(place == mine_row, 1.0, 0.0).astype(BF16)
    choose_sib = jnp.where(place == sib_row, 1.0, 0.0).astype(BF16)
    sib_copies = []
    rs_copies = []

    def send_sum(k):
        sib_copies[k].wait_recv()
        summed = mine[k] + sib_recv[k].astype(F32)
        mine[k] = summed
        rs_send[k] = summed.astype(BF16)
        for j in range(1, pairs):
            to = (pair + j) % pairs
            rows = pl.ds(pl.multiple_of(to * rows_cap, rows_cap), rows_cap)
            copy = remote(
                rs_send.at[k, rows], rs_recv.at[k, j], rs_s.at[k, j], rs_r.at[k, j], (ctx, to * 2 + core)
            )
            copy.start()
            rs_copies.append(copy)

    for k in range(n_cols):
        cols = slice(k * col, (k + 1) * col)
        by_token = dot(hid[...], cond_wv[:, cols]).astype(BF16)
        sib_send[k] = dot(choose_sib, by_token).astype(BF16)
        copy = remote(sib_send.at[k], sib_recv.at[k], sb_s.at[k], sb_r.at[k], (ctx, sibling))
        copy.start()
        sib_copies.append(copy)
        mine[k] = dot(choose_mine, by_token)
        if k:
            send_sum(k - 1)
    send_sum(n_cols - 1)

    squares = [jnp.zeros((rows_cap, 1), F32) for _ in range(draws)]
    for k in range(n_cols):
        cols = slice(k * col, (k + 1) * col)
        cond = mine[k, pl.ds(pl.multiple_of(pair * rows_cap, rows_cap), rows_cap), :]
        for j in range(1, pairs):
            rs_copies[k * (pairs - 1) + j - 1].wait_recv()
            cond = cond + rs_recv[k, j].astype(F32)
        for d in range(draws):
            rows = slice(d * rows_cap, (d + 1) * rows_cap)
            lifted = base[rows, cols] + cond
            base[rows, cols] = lifted
            squares[d] = squares[d] + jnp.sum(lifted * lifted, axis=1, keepdims=True)
    gain = row_of(gain_rows)
    for d in range(draws):
        rows = slice(d * rows_cap, (d + 1) * rows_cap)
        scale = lax.rsqrt(squares[d] / width + 1e-06)
        normed[rows, :] = (base[rows, :] * scale * gain).astype(BF16)
    loads[4].wait()

    def middle_cols(i, total):
        start = pl.multiple_of(i * 256, 256)
        middle = dot(normed[...], mid_wv[:, pl.ds(start, 256)])
        block = (base[:, pl.ds(start, 256)] + middle / (1.0 + jnp.exp(-middle))).astype(BF16)
        return total + lax.dot_general(
            block, noise_out[:, pl.ds(start, 256)], (((1,), (1,)), ((), ())), preferred_element_type=F32
        )

    result = lax.fori_loop(0, width // 256, middle_cols, jnp.zeros((draws * rows_cap, latent), F32))
    occupied = jnp.sum(own_slots(), axis=1, keepdims=True)
    for d in range(draws):
        block = result[d * rows_cap : (d + 1) * rows_cap] * occupied
        pred_out[:, d * latent : (d + 1) * latent] = block[:cap]

    for k in range(ROW_PARTS):
        forward(0, 0, k).wait_send()
        for way in (0, 1):
            for step in range(pairs - 1):

                @pl.when(sends(way, step))
                def _():
                    chain(way, step, k).wait_send()

                @pl.when(gets(way, step))
                def _():
                    forward(way, step + 1, k).wait_send()

    for copy in kv_copies + att_copies + att_fw + sib_copies + rs_copies:
        copy.wait_send()


def shards(n_ctx, n_grp, *arrays):
    (tokens, frames, qkv_w, out_w, cond_w, bias, in_w, mid_w, noise_out, gain) = arrays[:10]
    targets, noise, steps, masked, routes = arrays[10:]
    tok_rows, d_shard = tokens.shape
    head = qkv_w.shape[1] // 3
    width = in_w.shape[1]
    draws = steps.shape[1]
    pairs = n_grp // 2
    cap = max(2, 3 * tok_rows // (2 * n_grp))
    rows_cap = -(-cap // 16) * 16
    n_cols = 3
    col = width // n_cols
    half = width // 2
    freqs = np.exp(-math.log(10000.0) * np.arange(half, dtype=np.float32) / half).astype(np.float32)
    lanes = 128
    latent = targets.shape[1]
    vmem = pl.BlockSpec(memory_space=pltpu.VMEM)
    hbm = pl.BlockSpec(memory_space=pltpu.HBM)
    dma = pltpu.SemaphoreType.DMA
    chain = dma((2, pairs - 1, ROW_PARTS))
    fwd = dma((2, pairs, ROW_PARTS))
    ops = (
        tokens,
        frames.reshape(1, -1),
        qkv_w,
        out_w,
        cond_w,
        bias.reshape(-1, lanes),
        in_w,
        mid_w,
        noise_out.T,
        gain.reshape(-1, lanes),
        targets.T,
        noise.T,
        steps.T,
        masked.reshape(1, -1),
        routes.reshape(1, -1),
        jnp.asarray(freqs.reshape(-1, lanes)),
    )
    small = [pltpu.VMEM(ops[i].shape, ops[i].dtype) for i in (1, 5, 6, 8, 9, 10, 11, 12, 13, 14, 15)]
    return pl.pallas_call(
        functools.partial(kernel, n_ctx, n_grp, cap, rows_cap),
        out_shape=(
            jax.ShapeDtypeStruct(tokens.shape, BF16),
            jax.ShapeDtypeStruct((cap, noise.shape[1]), F32),
        ),
        in_specs=[hbm] * len(ops),
        out_specs=(vmem, vmem),
        scratch_shapes=[
            *small,
            pltpu.VMEM((n_grp, tok_rows, d_shard), BF16),
            pltpu.VMEM(qkv_w.shape, BF16),
            pltpu.VMEM(out_w.shape, BF16),
            pltpu.VMEM(cond_w.shape, BF16),
            pltpu.VMEM(mid_w.shape, BF16),
            pltpu.VMEM((n_ctx, tok_rows, 2 * head), BF16),
            pltpu.VMEM((tok_rows, head), BF16),
            pltpu.VMEM((tok_rows, n_grp * head), BF16),
            pltpu.VMEM((tok_rows, d_shard), BF16),
            pltpu.VMEM((tok_rows, 3 * head), F32),
            pltpu.VMEM((draws * rows_cap, width), F32),
            pltpu.VMEM((draws * rows_cap, width), BF16),
            pltpu.VMEM((rows_cap, draws), F32),
            pltpu.VMEM((draws * rows_cap, latent), BF16),
            pltpu.VMEM((1, tok_rows), jnp.int32),
            pltpu.VMEM((n_cols, pairs * rows_cap, col), F32),
            pltpu.VMEM((n_cols, pairs * rows_cap, col), BF16),
            pltpu.VMEM((n_cols, pairs * rows_cap, col), BF16),
            pltpu.VMEM((n_cols, pairs * rows_cap, col), BF16),
            pltpu.VMEM((n_cols, pairs, rows_cap, col), BF16),
            dma((5,)),
            dma((len(small),)),
            chain,
            chain,
            fwd,
            fwd,
            dma((n_ctx,)),
            dma((n_ctx,)),
            dma((pairs,)),
            dma((pairs,)),
            dma((pairs,)),
            dma((pairs,)),
            dma((n_cols,)),
            dma((n_cols,)),
            dma((n_cols, pairs)),
            dma((n_cols, pairs)),
        ],
        compiler_params=pltpu.CompilerParams(
            collective_id=0, has_side_effects=True, vmem_limit_bytes=64 * 2**20 - 2**16
        ),
    )(*ops)


def solution(mesh):
    return jax.shard_map(
        functools.partial(shards, mesh.shape["ctx"], mesh.shape["grp"]),
        mesh=mesh,
        in_specs=(
            P("ctx", "grp"),
            P(),
            P(None, "grp"),
            P(None, "grp"),
            P("grp", None),
            P(),
            P(),
            P(),
            P(),
            P(),
            P("ctx", None),
            P("ctx", None),
            P("ctx", None),
            P("ctx"),
            P("ctx", None),
        ),
        out_specs=(P("ctx", "grp"), P(("ctx", "grp"), None)),
        check_vma=False,
    )
```
